32 devices in a mesh: ctx: 8 (over y, x, core), head: 4 (over z).
Axes of the slice: x: 2, y: 2, z: 4, core: 2. Of those that a mesh axis runs over, the one named last changes fastest.
Arguments:
- queries: bfloat16 [2, 1536, 4096], P(None, 'ctx', 'head'), may hold values from -6 to 6
- key_rows: bfloat16 [2, 1536, 4096], P(None, 'ctx', 'head'), may hold values from -6 to 6
- value_rows: bfloat16 [2, 1536, 4096], P(None, 'ctx', 'head'), may hold values from -6 to 6
- out_weight: bfloat16 [4096, 4096], P('head'), may hold values from -0.09375 to 0.09375
- cotangent: bfloat16 [2, 1536, 4096], P(None, 'ctx', 'head'), may hold values from -6 to 6
Outputs:
- layer_output: bfloat16 [2, 1536, 4096], P(None, 'ctx', 'head')
- query_grad: bfloat16 [2, 1536, 4096], P(None, 'ctx', 'head')
- key_grad: bfloat16 [2, 1536, 4096], P(None, 'ctx', 'head')
- value_grad: bfloat16 [2, 1536, 4096], P(None, 'ctx', 'head')
- weight_grad: float32 [4096, 4096], P('head', 'ctx')
The draws below stay inside these ranges and needn't reach their ends.
All inputs are finite; a program needn't handle non-finite values.
Results may differ from the reference program's by a relative error of at most 0.015.
Values may be sent and summed in bfloat16 or wider, within the bound.
A program may use at most 128 MiB of HBM per device.

```python
import jax
import jax.numpy as jnp
from jax import lax

D = 4096
HEADS = 32
DH = 128
TOK_DEV = 192
HD = 4096
TOKENS = 1536
N_CTX = 8


def spiked(values, key, source, target, parts, factor):
    owner, partner = [(jnp.arange(values.shape[dim]) // (values.shape[dim] // parts)).reshape([-1 if axis == dim else 1 for axis in range(values.ndim)]) for dim in (source, target)]
    chosen = jax.random.permutation(key, parts)[partner]
    strong = (owner == chosen) | (owner == (partner + parts // 2) % parts)
    return jnp.where(strong, factor * values, values)


def block_scale(key, shape, shards, smallest, largest):
    loudness = 1.0
    for dim, parts in shards:
        steps = jax.random.uniform(jax.random.fold_in(jax.random.fold_in(key, 6), dim), (parts,), jnp.float32, smallest / len(shards), largest / len(shards))
        loudness = loudness * jnp.repeat(jnp.exp(steps), shape[dim] // parts).reshape((-1,) + (1,) * (len(shape) - 1 - dim))
    return loudness


def bell_draw(key, shape, scale, bound, cuts=(), dtype=jnp.bfloat16):
    entries = scale * jax.random.normal(key, shape, jnp.float32)
    if cuts:
        entries = entries * block_scale(key, shape, cuts, -0.22, 0.18)
    return jnp.clip(entries, -bound, bound).astype(dtype)


def noise_with(stream_key, extent, width, most, split, heavy, held_as=jnp.bfloat16):
    values = width * jax.random.normal(stream_key, extent, jnp.float32)
    if split:
        values = values * block_scale(stream_key, extent, split, -0.22, 0.18)
    return jnp.clip(spiked(values, jax.random.fold_in(stream_key, 3), *heavy), -most, most).astype(held_as)


def setup_inputs(seed: int = 0) -> dict:
    splits = jax.random.split(jax.random.key(seed), 6)
    queries = bell_draw(splits[0], (2, TOKENS, HD), 1.0, 6.0, ((1, 8), (2, 4)))
    key_rows = bell_draw(splits[1], (2, TOKENS, HD), 1.0, 6.0, ((1, 8), (2, 4)))
    value_rows = bell_draw(splits[2], (2, TOKENS, HD), 1.0, 6.0, ((1, 8), (2, 4)))
    out_weight = bell_draw(splits[3], (HD, D), HD ** -0.5, 0.09375, ((0, 4),))
    cotangent = noise_with(splits[4], (2, TOKENS, D), 1.0, 6.0, ((1, 8), (2, 4)), (1, 2, 8, 2.0))
    return {"queries": queries, "key_rows": key_rows, "value_rows": value_rows, "out_weight": out_weight, "cotangent": cotangent}


epsilon = 1e-06

def to_blocks(array):
    return array.reshape(2, N_CTX, TOK_DEV, HEADS, DH).transpose(1, 0, 3, 2, 4)

def from_blocks(array):
    return array.transpose(1, 0, 3, 2, 4).reshape(2, N_CTX * TOK_DEV, HEADS * DH)

def rms_normalize(attended):
    return attended / jnp.sqrt(lax.optimization_barrier(jnp.mean(attended * attended, axis=-1, keepdims=True)) + epsilon)

def causal_mask():
    rows_index = lax.broadcasted_iota(jnp.int32, (TOK_DEV, TOK_DEV), 0)
    cols_index = lax.broadcasted_iota(jnp.int32, (TOK_DEV, TOK_DEV), 1)
    return rows_index >= cols_index

def reference(queries, key_rows, value_rows, out_weight, cotangent):
    head_scale = DH ** (-0.5)
    lower = causal_mask()
    query_blocks = to_blocks(queries)
    key_blocks = to_blocks(key_rows)
    value_blocks = to_blocks(value_rows)

    def block_scores(query_block, key_block):
        raw = jnp.einsum('bhtd,bhsd->bhts', query_block.astype(jnp.float32), key_block.astype(jnp.float32)) * head_scale
        return jnp.where(lower, raw, 0.0).astype(jnp.bfloat16)

    def forward_step(carry, inputs):
        query_block, key_block, value_block = inputs
        scores = block_scores(query_block, key_block)
        state_bf = carry.astype(jnp.bfloat16).astype(jnp.float32)
        attended = jnp.einsum('bhts,bhsd->bhtd', scores.astype(jnp.float32), value_block.astype(jnp.float32))
        attended = attended + head_scale * jnp.einsum('bhtd,bhde->bhte', query_block.astype(jnp.float32), state_bf)
        updated = carry + jnp.einsum('bhsd,bhse->bhde', key_block.astype(jnp.float32), value_block.astype(jnp.float32))
        return (updated, (attended, carry))
    start_state = jnp.zeros((2, HEADS, DH, DH), jnp.float32)
    final_state, (attended, states) = lax.scan(forward_step, start_state, (query_blocks, key_blocks, value_blocks))
    normed = from_blocks(rms_normalize(attended).astype(jnp.bfloat16))
    normed_flat = normed.reshape(2 * TOKENS, HD)
    layer_output = jnp.dot(normed_flat, out_weight, preferred_element_type=jnp.float32).astype(jnp.bfloat16).reshape(2, TOKENS, D)
    grad_flat = cotangent.reshape(2 * TOKENS, D)
    normed_grad = jnp.dot(grad_flat, out_weight.T, preferred_element_type=jnp.float32).reshape(2, TOKENS, HD)
    weight_grad = jnp.dot(normed_flat.T, grad_flat, preferred_element_type=jnp.float32) * (2 * TOKENS) ** (-0.5)
    pullback = jax.vjp(rms_normalize, attended)[1]
    attended_grad = pullback(to_blocks(normed_grad))[0].astype(jnp.bfloat16)

    def backward_step(carry, inputs):
        query_block, key_block, value_block, grad_block, state = inputs
        scores = block_scores(query_block, key_block).astype(jnp.float32)
        grad_f = grad_block.astype(jnp.float32)
        query_f = query_block.astype(jnp.float32)
        key_f = key_block.astype(jnp.float32)
        value_f = value_block.astype(jnp.float32)
        raw = jnp.einsum('bhtd,bhsd->bhts', grad_f, value_f) * head_scale
        score_grad = jnp.where(lower, raw, 0.0).astype(jnp.bfloat16).astype(jnp.float32)
        state_bf = state.astype(jnp.bfloat16).astype(jnp.float32)
        grad_state_bf = carry.astype(jnp.bfloat16).astype(jnp.float32)
        query_part = jnp.einsum('bhts,bhsd->bhtd', score_grad, key_f) + head_scale * jnp.einsum('bhte,bhde->bhtd', grad_f, state_bf)
        key_part = jnp.einsum('bhts,bhtd->bhsd', score_grad, query_f) + head_scale * jnp.einsum('bhse,bhde->bhsd', value_f, grad_state_bf)
        value_part = jnp.einsum('bhts,bhte->bhse', scores, grad_f) + head_scale * jnp.einsum('bhsd,bhde->bhse', key_f, grad_state_bf)
        updated = carry + jnp.einsum('bhtd,bhte->bhde', query_f, grad_f)
        return (updated, (query_part.astype(jnp.bfloat16), key_part.astype(jnp.bfloat16), value_part.astype(jnp.bfloat16)))
    last_grad, (query_grad, key_grad, value_grad) = lax.scan(backward_step, start_state, (query_blocks, key_blocks, value_blocks, attended_grad, states), reverse=True)
    return (layer_output, from_blocks(query_grad), from_blocks(key_grad), from_blocks(value_grad), weight_grad)
```

```python
import jax
import jax.numpy as jnp
from jax import lax
from jax.sharding import PartitionSpec as P

DH = 128


epsilon = 1e-06


def swap(array, axis, bit):
    count = lax.axis_size(axis)
    return lax.ppermute(array, axis, [(i, i ^ bit) for i in range(count)])


def exclusive_scan(part, axis, reverse):
    count = lax.axis_size(axis)
    place = lax.axis_index(axis)
    core = place % 2
    other = swap(part.astype(jnp.bfloat16), axis, 1).astype(jnp.float32)
    total = lax.dynamic_index_in_dim(part + other, core, 0, False)
    before = jnp.zeros_like(total)
    bit = 2
    while bit < count:
        came = swap(total.astype(jnp.bfloat16), axis, bit).astype(jnp.float32)
        mine = (place // bit) % 2
        takes = (mine == 0) if reverse else (mine == 1)
        before = before + jnp.where(takes, came, 0.0)
        total = total + came
        bit *= 2
    before = before.astype(jnp.bfloat16)
    came = swap(before, axis, 1)
    first = jnp.where(core == 0, before, came)
    second = jnp.where(core == 0, came, before)
    pairs = jnp.stack([first, second]).astype(jnp.float32)
    takes = (core == 0) if reverse else (core == 1)
    return pairs + jnp.where(takes, other, 0.0)


def right_of(array, axis, first, last):
    return lax.ppermute(array, axis, [(i, i + 1) for i in range(first, last)])


def left_of(array, axis, first, last):
    return lax.ppermute(array, axis, [(i, i - 1) for i in range(first, last)])


def gather_line(block, axis):
    count = lax.axis_size(axis)
    place = lax.axis_index(axis)
    from_left, from_right = block, block
    lefts, rights = {}, {}
    for step in range(1, count):
        from_left = right_of(from_left, axis, step - 1, count - 1)
        from_right = left_of(from_right, axis, 1, count - step + 1)
        lefts[step], rights[step] = from_left, from_right
    blocks = [block]
    for offset in range(1, count):
        blocks.append(
            jnp.where(place + offset < count, rights[offset], lefts[count - offset])
        )
    return blocks


def scatter_line(terms, axis):
    count = lax.axis_size(axis)
    rightward = leftward = None
    for step in range(1, count):
        to_right, to_left = terms[count - step], terms[step]
        if rightward is not None:
            to_right = to_right + rightward.astype(jnp.float32)
            to_left = to_left + leftward.astype(jnp.float32)
        rightward = right_of(to_right.astype(jnp.bfloat16), axis, 0, step)
        leftward = left_of(to_left.astype(jnp.bfloat16), axis, count - step, count)
    return terms[0] + rightward.astype(jnp.float32) + leftward.astype(jnp.float32)


def halve(blocks, axis, bits):
    for bit in bits:
        sent = {
            k: swap(block.astype(jnp.bfloat16), axis, bit)
            for k, block in blocks.items()
            if k & bit
        }
        blocks = {
            k: block + sent[k | bit].astype(jnp.float32)
            for k, block in blocks.items()
            if not k & bit
        }
    return blocks


def split_heads(array):
    length = array.shape[1]
    return array.reshape(2, length, array.shape[2] // DH, DH).transpose(0, 2, 1, 3)


def join_heads(array):
    length = array.shape[2]
    return array.transpose(0, 2, 1, 3).reshape(2, length, array.shape[1] * DH)


def rms_normalize(attended):
    return attended / jnp.sqrt(jnp.mean(attended * attended, axis=-1, keepdims=True) + epsilon)


def shards(queries, key_rows, value_rows, out_weight, cotangent):
    head_scale = DH ** (-0.5)
    length = queries.shape[1]
    rows_index = lax.broadcasted_iota(jnp.int32, (length, length), 0)
    cols_index = lax.broadcasted_iota(jnp.int32, (length, length), 1)
    lower = rows_index >= cols_index
    query_heads = split_heads(queries)
    key_heads = split_heads(key_rows)
    value_heads = split_heads(value_rows)
    raw = (
        jnp.einsum("bhtd,bhsd->bhts", query_heads, key_heads, preferred_element_type=jnp.float32)
        * head_scale
    )
    scores = jnp.where(lower, raw, 0.0).astype(jnp.bfloat16)
    local_state = jnp.einsum(
        "bhsd,bhse->bhde", key_heads, value_heads, preferred_element_type=jnp.float32
    )
    state = exclusive_scan(local_state, "ctx", False)
    state_bf = state.astype(jnp.bfloat16)
    attended = jnp.einsum(
        "bhts,bhsd->bhtd", scores, value_heads, preferred_element_type=jnp.float32
    )
    attended = attended + head_scale * jnp.einsum(
        "bhtd,bhde->bhte", query_heads, state_bf, preferred_element_type=jnp.float32
    )
    normed_flat = join_heads(rms_normalize(attended).astype(jnp.bfloat16))
    groups = lax.axis_size("head")
    group = lax.axis_index("head")
    width = cotangent.shape[2]
    columns = [
        lax.dynamic_slice_in_dim(out_weight, (group + o) % groups * width, width, 1)
        for o in range(groups)
    ]
    grads = gather_line(cotangent, "head")
    layer_output = scatter_line(
        [
            jnp.einsum("btr,rc->btc", normed_flat, part, preferred_element_type=jnp.float32)
            for part in columns
        ],
        "head",
    ).astype(jnp.bfloat16)
    normed_grad = sum(
        jnp.einsum("btc,rc->btr", grad, part, preferred_element_type=jnp.float32)
        for grad, part in zip(grads, columns)
    )
    places = lax.axis_size("ctx")
    place = lax.axis_index("ctx")
    span = groups * width // places
    grad_all = jnp.concatenate(grads, axis=2)
    blocks = {}
    for k in range(places):
        start = ((place ^ k) * span - group * width) % (groups * width)
        wanted = lax.dynamic_slice_in_dim(grad_all, start, span, 2)
        blocks[k] = jnp.einsum(
            "btr,btc->rc", normed_flat, wanted, preferred_element_type=jnp.float32
        )
    blocks = halve(blocks, "ctx", [1])
    bits = [1 << i for i in range(1, places.bit_length() - 1)]
    rows = normed_flat.shape[2] // 2
    upper = halve({k: block[:rows] for k, block in blocks.items()}, "ctx", bits)
    lower_rows = halve({k: block[rows:] for k, block in blocks.items()}, "ctx", bits[::-1])
    token_factor = (2 * length * places) ** (-0.5)
    weight_grad = jnp.concatenate([upper[0], lower_rows[0]], axis=0) * token_factor
    pullback = jax.vjp(rms_normalize, attended)[1]
    attended_grad = pullback(split_heads(normed_grad))[0].astype(jnp.bfloat16)
    local_grad_state = jnp.einsum(
        "bhtd,bhte->bhde", query_heads, attended_grad, preferred_element_type=jnp.float32
    )
    grad_state = exclusive_scan(local_grad_state, "ctx", True)
    grad_state_bf = grad_state.astype(jnp.bfloat16)
    raw_grad = (
        jnp.einsum(
            "bhtd,bhsd->bhts", attended_grad, value_heads, preferred_element_type=jnp.float32
        )
        * head_scale
    )
    score_grad = jnp.where(lower, raw_grad, 0.0).astype(jnp.bfloat16)
    query_part = jnp.einsum(
        "bhts,bhsd->bhtd", score_grad, key_heads, preferred_element_type=jnp.float32
    )
    query_part = query_part + head_scale * jnp.einsum(
        "bhte,bhde->bhtd", attended_grad, state_bf, preferred_element_type=jnp.float32
    )
    key_part = jnp.einsum(
        "bhts,bhtd->bhsd", score_grad, query_heads, preferred_element_type=jnp.float32
    )
    key_part = key_part + head_scale * jnp.einsum(
        "bhse,bhde->bhsd", value_heads, grad_state_bf, preferred_element_type=jnp.float32
    )
    value_part = jnp.einsum(
        "bhts,bhte->bhse", scores, attended_grad, preferred_element_type=jnp.float32
    )
    value_part = value_part + head_scale * jnp.einsum(
        "bhsd,bhde->bhse", key_heads, grad_state_bf, preferred_element_type=jnp.float32
    )
    query_grad = join_heads(query_part.astype(jnp.bfloat16))
    key_grad = join_heads(key_part.astype(jnp.bfloat16))
    value_grad = join_heads(value_part.astype(jnp.bfloat16))
    return (layer_output, query_grad, key_grad, value_grad, weight_grad)


def solution(mesh):
    in_specs = (
        P(None, "ctx", "head"),
        P(None, "ctx", "head"),
        P(None, "ctx", "head"),
        P("head", None),
        P(None, "ctx", "head"),
    )
    out_specs = (
        P(None, "ctx", "head"),
        P(None, "ctx", "head"),
        P(None, "ctx", "head"),
        P(None, "ctx", "head"),
        P("head", "ctx"),
    )
    return jax.shard_map(shards, mesh=mesh, in_specs=in_specs, out_specs=out_specs, check_vma=False)
```

```python
import jax
import jax.numpy as jnp
from jax import lax
from jax.sharding import PartitionSpec as P

DH = 128


epsilon = 1e-06


def swap(array, axis, bit):
    count = lax.axis_size(axis)
    return lax.ppermute(array, axis, [(i, i ^ bit) for i in range(count)])


def exclusive_scan(part, axis, reverse, beside=()):
    count = lax.axis_size(axis)
    place = lax.axis_index(axis)
    core = place % 2
    other = swap(part.astype(jnp.bfloat16), axis, 1).astype(jnp.float32)
    total = lax.dynamic_index_in_dim(part + other, core, 0, False)
    before = jnp.zeros_like(total)
    bit = 2
    while bit < count:
        came = swap(total.astype(jnp.bfloat16), axis, bit).astype(jnp.float32)
        mine = (place // bit) % 2
        takes = (mine == 0) if reverse else (mine == 1)
        before = before + jnp.where(takes, came, 0.0)
        total = total + came
        bit *= 2
    before, beside = lax.optimization_barrier((before.astype(jnp.bfloat16), beside))
    came = swap(before, axis, 1)
    first = jnp.where(core == 0, before, came)
    second = jnp.where(core == 0, came, before)
    pairs = jnp.stack([first, second]).astype(jnp.float32)
    takes = (core == 0) if reverse else (core == 1)
    return pairs + jnp.where(takes, other, 0.0), beside


def right_of(array, axis, first, last):
    return lax.ppermute(array, axis, [(i, i + 1) for i in range(first, last)])


def left_of(array, axis, first, last):
    return lax.ppermute(array, axis, [(i, i - 1) for i in range(first, last)])


def line_order(count):
    table = []
    for place in range(count):
        entries = []
        for block in range(count):
            entries.append((abs(block - place), int(block > place), block))
        table.append(sorted(entries))
    return table


def look_up(values, place):
    out = jnp.int32(values[0])
    for i, value in enumerate(values[1:], 1):
        out = jnp.where(place == i, value, out)
    return out


def gather_step(came, axis, step):
    count = lax.axis_size(axis)
    return (
        right_of(came[0], axis, step - 1, count - 1),
        left_of(came[1], axis, 1, count - step + 1),
    )


def pick(arrived, rank, table, place):
    choices = {}
    for i, row in enumerate(table):
        choices.setdefault(row[rank][:2], []).append(i)
    out = None
    for (distance, side), owners in choices.items():
        block = arrived[distance][side]
        if out is None:
            out = block
        else:
            wanted = place == owners[0]
            for owner in owners[1:]:
                wanted = wanted | (place == owner)
            out = jnp.where(wanted, block, out)
    return out


def scatter_step(terms, came, axis, step):
    count = lax.axis_size(axis)
    to_right, to_left = terms[count - step], terms[step]
    if came is not None:
        to_right = to_right + came[0].astype(jnp.float32)
        to_left = to_left + came[1].astype(jnp.float32)
    return (
        right_of(to_right.astype(jnp.bfloat16), axis, 0, step),
        left_of(to_left.astype(jnp.bfloat16), axis, count - step, count),
    )


def halve(blocks, axis, bits):
    for bit in bits:
        sent = {
            k: swap(block.astype(jnp.bfloat16), axis, bit)
            for k, block in blocks.items()
            if k & bit
        }
        blocks = {
            k: block + sent[k | bit].astype(jnp.float32)
            for k, block in blocks.items()
            if not k & bit
        }
    return blocks


def split_heads(array):
    length = array.shape[1]
    return array.reshape(2, length, array.shape[2] // DH, DH).transpose(0, 2, 1, 3)


def join_heads(array):
    length = array.shape[2]
    return array.transpose(0, 2, 1, 3).reshape(2, length, array.shape[1] * DH)


def rms_normalize(attended):
    return attended / jnp.sqrt(jnp.mean(attended * attended, axis=-1, keepdims=True) + epsilon)


def shards(queries, key_rows, value_rows, out_weight, cotangent):
    head_scale = DH ** (-0.5)
    length = queries.shape[1]
    rows_index = lax.broadcasted_iota(jnp.int32, (length, length), 0)
    cols_index = lax.broadcasted_iota(jnp.int32, (length, length), 1)
    lower = rows_index >= cols_index
    groups = lax.axis_size("head")
    group = lax.axis_index("head")
    arrived = {0: (cotangent, cotangent)}
    arrived[1] = gather_step(arrived[0], "head", 1)
    query_heads = split_heads(queries)
    key_heads = split_heads(key_rows)
    value_heads = split_heads(value_rows)
    raw = (
        jnp.einsum("bhtd,bhsd->bhts", query_heads, key_heads, preferred_element_type=jnp.float32)
        * head_scale
    )
    scores = jnp.where(lower, raw, 0.0).astype(jnp.bfloat16)
    local_state = jnp.einsum(
        "bhsd,bhse->bhde", key_heads, value_heads, preferred_element_type=jnp.float32
    )
    state, arrived[1] = exclusive_scan(local_state, "ctx", False, arrived[1])
    for step in range(2, groups):
        arrived[step] = gather_step(arrived[step - 1], "head", step)
    state_bf = state.astype(jnp.bfloat16)
    attended = jnp.einsum(
        "bhts,bhsd->bhtd", scores, value_heads, preferred_element_type=jnp.float32
    )
    attended = attended + head_scale * jnp.einsum(
        "bhtd,bhde->bhte", query_heads, state_bf, preferred_element_type=jnp.float32
    )
    normed_flat = join_heads(rms_normalize(attended).astype(jnp.bfloat16))
    width = cotangent.shape[2]
    terms = [
        jnp.einsum(
            "btr,rc->btc",
            normed_flat,
            lax.dynamic_slice_in_dim(out_weight, (group + o) % groups * width, width, 1),
            preferred_element_type=jnp.float32,
        )
        for o in range(groups)
    ]
    came_out = scatter_step(terms, None, "head", 1)
    places = lax.axis_size("ctx")
    core = lax.axis_index("ctx") % 2
    span = groups * width // places
    chips = places // 2
    table = line_order(groups)
    per = chips // groups
    normed_grad = 0.0
    pair_sums = []
    for rank in range(groups):
        block = look_up([row[rank][2] for row in table], group)
        grad = pick(arrived, rank, table, group)
        if rank == groups - 1:
            grad, pair_sums, came_out = lax.optimization_barrier((grad, pair_sums, came_out))
        columns = lax.dynamic_slice_in_dim(out_weight, block * width, width, 1)
        normed_grad = normed_grad + jnp.einsum(
            "btc,rc->btr", grad, columns, preferred_element_type=jnp.float32
        )
        for t in range(per):
            theirs, ours = [
                jnp.einsum(
                    "btr,btc->rc",
                    normed_flat,
                    lax.dynamic_slice_in_dim(grad, (2 * t + side) * span, span, 2),
                    preferred_element_type=jnp.float32,
                )
                for side in (1 - core, core)
            ]
            came = swap(theirs.astype(jnp.bfloat16), "ctx", 1)
            pair_sums.append((ours + came.astype(jnp.float32)).astype(jnp.bfloat16))
    pullback = jax.vjp(rms_normalize, attended)[1]
    attended_grad = pullback(split_heads(normed_grad))[0].astype(jnp.bfloat16)
    local_grad_state = jnp.einsum(
        "bhtd,bhte->bhde", query_heads, attended_grad, preferred_element_type=jnp.float32
    )
    pair_sums = jnp.stack(pair_sums)
    for step in range(2, groups - 1):
        came_out = scatter_step(terms, came_out, "head", step)
    grad_state, (pair_sums, came_out) = exclusive_scan(
        local_grad_state, "ctx", True, (pair_sums, came_out)
    )
    came_out = scatter_step(terms, came_out, "head", groups - 1)
    layer_output = (
        terms[0] + came_out[0].astype(jnp.float32) + came_out[1].astype(jnp.float32)
    ).astype(jnp.bfloat16)
    chip = lax.axis_index("ctx") // 2
    positions = [[[e[2] for e in row].index(g) for row in table] for g in range(groups)]
    blocks = {}
    for k in range(chips):
        wanted = chip ^ k
        rank = jnp.int32(0)
        for g in range(groups):
            rank = jnp.where(wanted // per == g, look_up(positions[g], group), rank)
        blocks[2 * k] = lax.dynamic_index_in_dim(
            pair_sums, rank * per + wanted % per, 0, False
        ).astype(jnp.float32)
    bits = [1 << i for i in range(1, places.bit_length() - 1)]
    rows = normed_flat.shape[2] // 2
    upper = halve({k: block[:rows] for k, block in blocks.items()}, "ctx", bits)
    lower_rows = halve({k: block[rows:] for k, block in blocks.items()}, "ctx", bits[::-1])
    token_factor = (2 * length * places) ** (-0.5)
    weight_grad = jnp.concatenate([upper[0], lower_rows[0]], axis=0) * token_factor
    grad_state_bf = grad_state.astype(jnp.bfloat16)
    raw_grad = (
        jnp.einsum(
            "bhtd,bhsd->bhts", attended_grad, value_heads, preferred_element_type=jnp.float32
        )
        * head_scale
    )
    score_grad = jnp.where(lower, raw_grad, 0.0).astype(jnp.bfloat16)
    query_part = jnp.einsum(
        "bhts,bhsd->bhtd", score_grad, key_heads, preferred_element_type=jnp.float32
    )
    query_part = query_part + head_scale * jnp.einsum(
        "bhte,bhde->bhtd", attended_grad, state_bf, preferred_element_type=jnp.float32
    )
    key_part = jnp.einsum(
        "bhts,bhtd->bhsd", score_grad, query_heads, preferred_element_type=jnp.float32
    )
    key_part = key_part + head_scale * jnp.einsum(
        "bhse,bhde->bhsd", value_heads, grad_state_bf, preferred_element_type=jnp.float32
    )
    value_part = jnp.einsum(
        "bhts,bhte->bhse", scores, attended_grad, preferred_element_type=jnp.float32
    )
    value_part = value_part + head_scale * jnp.einsum(
        "bhsd,bhde->bhse", key_heads, grad_state_bf, preferred_element_type=jnp.float32
    )
    query_grad = join_heads(query_part.astype(jnp.bfloat16))
    key_grad = join_heads(key_part.astype(jnp.bfloat16))
    value_grad = join_heads(value_part.astype(jnp.bfloat16))
    return (layer_output, query_grad, key_grad, value_grad, weight_grad)


def solution(mesh):
    in_specs = (
        P(None, "ctx", "head"),
        P(None, "ctx", "head"),
        P(None, "ctx", "head"),
        P("head", None),
        P(None, "ctx", "head"),
    )
    out_specs = (
        P(None, "ctx", "head"),
        P(None, "ctx", "head"),
        P(None, "ctx", "head"),
        P(None, "ctx", "head"),
        P("head", "ctx"),
    )
    return jax.shard_map(shards, mesh=mesh, in_specs=in_specs, out_specs=out_specs, check_vma=False)
```

```python
import jax
import jax.numpy as jnp
from jax import lax
from jax.sharding import PartitionSpec as P

DH = 128


epsilon = 1e-06


def swap(array, axis, bit):
    count = lax.axis_size(axis)
    return lax.ppermute(array, axis, [(i, i ^ bit) for i in range(count)])


def exclusive_scan(part, axis, reverse, beside=()):
    count = lax.axis_size(axis)
    place = lax.axis_index(axis)
    core = place % 2
    other = swap(part.astype(jnp.bfloat16), axis, 1).astype(jnp.float32)
    total = lax.dynamic_index_in_dim(part + other, core, 0, False)
    before = jnp.zeros_like(total)
    bit = 2
    while bit < count:
        came = swap(total.astype(jnp.bfloat16), axis, bit).astype(jnp.float32)
        mine = (place // bit) % 2
        takes = (mine == 0) if reverse else (mine == 1)
        before = before + jnp.where(takes, came, 0.0)
        total = total + came
        bit *= 2
    before, beside = lax.optimization_barrier((before.astype(jnp.bfloat16), beside))
    came = swap(before, axis, 1)
    first = jnp.where(core == 0, before, came)
    second = jnp.where(core == 0, came, before)
    pairs = jnp.stack([first, second]).astype(jnp.float32)
    takes = (core == 0) if reverse else (core == 1)
    return pairs + jnp.where(takes, other, 0.0), beside


def right_of(array, axis, first, last):
    return lax.ppermute(array, axis, [(i, i + 1) for i in range(first, last)])


def left_of(array, axis, first, last):
    return lax.ppermute(array, axis, [(i, i - 1) for i in range(first, last)])


def line_order(count):
    table = []
    for place in range(count):
        entries = []
        for block in range(count):
            entries.append((abs(block - place), int(block > place), block))
        table.append(sorted(entries))
    return table


def look_up(values, place):
    out = jnp.int32(values[0])
    for i, value in enumerate(values[1:], 1):
        out = jnp.where(place == i, value, out)
    return out


def gather_step(came, axis, step):
    count = lax.axis_size(axis)
    return (
        right_of(came[0], axis, step - 1, count - 1),
        left_of(came[1], axis, 1, count - step + 1),
    )


def pick(arrived, rank, table, place):
    choices = {}
    for i, row in enumerate(table):
        choices.setdefault(row[rank][:2], []).append(i)
    out = None
    for (distance, side), owners in choices.items():
        block = arrived[distance][side]
        if out is None:
            out = block
        else:
            wanted = place == owners[0]
            for owner in owners[1:]:
                wanted = wanted | (place == owner)
            out = jnp.where(wanted, block, out)
    return out


def scatter_step(terms, came, axis, step):
    count = lax.axis_size(axis)
    to_right, to_left = terms[count - step], terms[step]
    if came is not None:
        to_right = to_right + came[0].astype(jnp.float32)
        to_left = to_left + came[1].astype(jnp.float32)
    return (
        right_of(to_right.astype(jnp.bfloat16), axis, 0, step),
        left_of(to_left.astype(jnp.bfloat16), axis, count - step, count),
    )


def halve(blocks, axis, bits):
    for bit in bits:
        sent = {
            k: swap(block.astype(jnp.bfloat16), axis, bit)
            for k, block in blocks.items()
            if k & bit
        }
        blocks = {
            k: block + sent[k | bit].astype(jnp.float32)
            for k, block in blocks.items()
            if not k & bit
        }
    return blocks


def split_heads(array):
    length = array.shape[1]
    return array.reshape(2, length, array.shape[2] // DH, DH).transpose(0, 2, 1, 3)


def join_heads(array):
    length = array.shape[2]
    return array.transpose(0, 2, 1, 3).reshape(2, length, array.shape[1] * DH)


def rms_normalize(attended):
    return attended / jnp.sqrt(jnp.mean(attended * attended, axis=-1, keepdims=True) + epsilon)


def shards(queries, key_rows, value_rows, out_weight, cotangent):
    head_scale = DH ** (-0.5)
    length = queries.shape[1]
    rows_index = lax.broadcasted_iota(jnp.int32, (length, length), 0)
    cols_index = lax.broadcasted_iota(jnp.int32, (length, length), 1)
    lower = rows_index >= cols_index
    groups = lax.axis_size("head")
    group = lax.axis_index("head")
    arrived = {0: (cotangent, cotangent)}
    arrived[1] = gather_step(arrived[0], "head", 1)
    query_heads = split_heads(queries)
    key_heads = split_heads(key_rows)
    value_heads = split_heads(value_rows)
    raw = (
        jnp.einsum("bhtd,bhsd->bhts", query_heads, key_heads, preferred_element_type=jnp.float32)
        * head_scale
    )
    scores = jnp.where(lower, raw, 0.0).astype(jnp.bfloat16)
    local_state = jnp.einsum(
        "bhsd,bhse->bhde", key_heads, value_heads, preferred_element_type=jnp.float32
    )
    state, _ = exclusive_scan(local_state, "ctx", False)
    for step in range(2, groups):
        arrived[step] = gather_step(arrived[step - 1], "head", step)
    state_bf = state.astype(jnp.bfloat16)
    attended = jnp.einsum(
        "bhts,bhsd->bhtd", scores, value_heads, preferred_element_type=jnp.float32
    )
    attended = attended + head_scale * jnp.einsum(
        "bhtd,bhde->bhte", query_heads, state_bf, preferred_element_type=jnp.float32
    )
    normed_flat = join_heads(rms_normalize(attended).astype(jnp.bfloat16))
    width = cotangent.shape[2]
    terms = [
        jnp.einsum(
            "btr,rc->btc",
            normed_flat,
            lax.dynamic_slice_in_dim(out_weight, (group + o) % groups * width, width, 1),
            preferred_element_type=jnp.float32,
        )
        for o in range(groups)
    ]
    came_out = scatter_step(terms, None, "head", 1)
    places = lax.axis_size("ctx")
    core = lax.axis_index("ctx") % 2
    span = groups * width // places
    chips = places // 2
    table = line_order(groups)
    per = chips // groups
    normed_grad = 0.0
    pair_sums = []
    for rank in range(groups):
        block = look_up([row[rank][2] for row in table], group)
        if rank == groups - 1:
            arrived, pair_sums, came_out = lax.optimization_barrier(
                (arrived, pair_sums, came_out)
            )
        grad = pick(arrived, rank, table, group)
        columns = lax.dynamic_slice_in_dim(out_weight, block * width, width, 1)
        normed_grad = normed_grad + jnp.einsum(
            "btc,rc->btr", grad, columns, preferred_element_type=jnp.float32
        )
        for t in range(per):
            theirs, ours = [
                jnp.einsum(
                    "btr,btc->rc",
                    normed_flat,
                    lax.dynamic_slice_in_dim(grad, (2 * t + side) * span, span, 2),
                    preferred_element_type=jnp.float32,
                )
                for side in (1 - core, core)
            ]
            came = swap(theirs.astype(jnp.bfloat16), "ctx", 1)
            pair_sums.append((ours + came.astype(jnp.float32)).astype(jnp.bfloat16))
    pullback = jax.vjp(rms_normalize, attended)[1]
    attended_grad = pullback(split_heads(normed_grad))[0].astype(jnp.bfloat16)
    local_grad_state = jnp.einsum(
        "bhtd,bhte->bhde", query_heads, attended_grad, preferred_element_type=jnp.float32
    )
    pair_sums = jnp.stack(pair_sums)
    chip = lax.axis_index("ctx") // 2
    positions = [[[e[2] for e in row].index(g) for row in table] for g in range(groups)]
    blocks = {}
    for k in range(chips):
        wanted = chip ^ k
        rank = jnp.int32(0)
        for g in range(groups):
            rank = jnp.where(wanted // per == g, look_up(positions[g], group), rank)
        blocks[2 * k] = lax.dynamic_index_in_dim(
            pair_sums, rank * per + wanted % per, 0, False
        ).astype(jnp.float32)
    bits = [1 << i for i in range(1, places.bit_length() - 1)]
    rows = normed_flat.shape[2] // 2
    upper = halve({k: block[:rows] for k, block in blocks.items()}, "ctx", bits[:1])
    downer = halve({k: block[rows:] for k, block in blocks.items()}, "ctx", bits[::-1][:1])
    for step in range(2, groups - 1):
        came_out = scatter_step(terms, came_out, "head", step)
    grad_state, (upper, downer, came_out) = exclusive_scan(
        local_grad_state, "ctx", True, (upper, downer, came_out)
    )
    upper = halve(upper, "ctx", bits[1:])
    downer = halve(downer, "ctx", bits[::-1][1:])
    token_factor = (2 * length * places) ** (-0.5)
    weight_grad = jnp.concatenate([upper[0], downer[0]], axis=0) * token_factor
    came_out = scatter_step(terms, came_out, "head", groups - 1)
    layer_output = (
        terms[0] + came_out[0].astype(jnp.float32) + came_out[1].astype(jnp.float32)
    ).astype(jnp.bfloat16)
    grad_state_bf = grad_state.astype(jnp.bfloat16)
    raw_grad = (
        jnp.einsum(
            "bhtd,bhsd->bhts", attended_grad, value_heads, preferred_element_type=jnp.float32
        )
        * head_scale
    )
    score_grad = jnp.where(lower, raw_grad, 0.0).astype(jnp.bfloat16)
    query_part = jnp.einsum(
        "bhts,bhsd->bhtd", score_grad, key_heads, preferred_element_type=jnp.float32
    )
    query_part = query_part + head_scale * jnp.einsum(
        "bhte,bhde->bhtd", attended_grad, state_bf, preferred_element_type=jnp.float32
    )
    key_part = jnp.einsum(
        "bhts,bhtd->bhsd", score_grad, query_heads, preferred_element_type=jnp.float32
    )
    key_part = key_part + head_scale * jnp.einsum(
        "bhse,bhde->bhsd", value_heads, grad_state_bf, preferred_element_type=jnp.float32
    )
    value_part = jnp.einsum(
        "bhts,bhte->bhse", scores, attended_grad, preferred_element_type=jnp.float32
    )
    value_part = value_part + head_scale * jnp.einsum(
        "bhsd,bhde->bhse", key_heads, grad_state_bf, preferred_element_type=jnp.float32
    )
    query_grad = join_heads(query_part.astype(jnp.bfloat16))
    key_grad = join_heads(key_part.astype(jnp.bfloat16))
    value_grad = join_heads(value_part.astype(jnp.bfloat16))
    return (layer_output, query_grad, key_grad, value_grad, weight_grad)


def solution(mesh):
    in_specs = (
        P(None, "ctx", "head"),
        P(None, "ctx", "head"),
        P(None, "ctx", "head"),
        P("head", None),
        P(None, "ctx", "head"),
    )
    out_specs = (
        P(None, "ctx", "head"),
        P(None, "ctx", "head"),
        P(None, "ctx", "head"),
        P(None, "ctx", "head"),
        P("head", "ctx"),
    )
    return jax.shard_map(shards, mesh=mesh, in_specs=in_specs, out_specs=out_specs, check_vma=False)
```

```python
import jax
import jax.numpy as jnp
from jax import lax
from jax.sharding import PartitionSpec as P

DH = 128


epsilon = 1e-06


def swap(array, axis, bit):
    count = lax.axis_size(axis)
    return lax.ppermute(array, axis, [(i, i ^ bit) for i in range(count)])


def exclusive_scan(part, axis, reverse, beside=()):
    count = lax.axis_size(axis)
    place = lax.axis_index(axis)
    core = place % 2
    other = swap(part.astype(jnp.bfloat16), axis, 1).astype(jnp.float32)
    total = lax.dynamic_index_in_dim(part + other, core, 0, False)
    before = jnp.zeros_like(total)
    bit = 2
    while bit < count:
        came = swap(total.astype(jnp.bfloat16), axis, bit).astype(jnp.float32)
        mine = (place // bit) % 2
        takes = (mine == 0) if reverse else (mine == 1)
        before = before + jnp.where(takes, came, 0.0)
        total = total + came
        bit *= 2
    before, beside = lax.optimization_barrier((before.astype(jnp.bfloat16), beside))
    came = swap(before, axis, 1)
    first = jnp.where(core == 0, before, came)
    second = jnp.where(core == 0, came, before)
    pairs = jnp.stack([first, second]).astype(jnp.float32)
    takes = (core == 0) if reverse else (core == 1)
    return pairs + jnp.where(takes, other, 0.0), beside


def right_of(array, axis, first, last):
    return lax.ppermute(array, axis, [(i, i + 1) for i in range(first, last)])


def left_of(array, axis, first, last):
    return lax.ppermute(array, axis, [(i, i - 1) for i in range(first, last)])


def line_order(count):
    table = []
    for place in range(count):
        entries = []
        for block in range(count):
            entries.append((abs(block - place), int(block > place), block))
        table.append(sorted(entries))
    return table


def look_up(values, place):
    out = jnp.int32(values[0])
    for i, value in enumerate(values[1:], 1):
        out = jnp.where(place == i, value, out)
    return out


def gather_step(came, axis, step):
    count = lax.axis_size(axis)
    return (
        right_of(came[0], axis, step - 1, count - 1),
        left_of(came[1], axis, 1, count - step + 1),
    )


def pick(arrived, rank, table, place):
    choices = {}
    for i, row in enumerate(table):
        choices.setdefault(row[rank][:2], []).append(i)
    out = None
    for (distance, side), owners in choices.items():
        block = arrived[distance][side]
        if out is None:
            out = block
        else:
            wanted = place == owners[0]
            for owner in owners[1:]:
                wanted = wanted | (place == owner)
            out = jnp.where(wanted, block, out)
    return out


def scatter_step(terms, came, axis, step):
    count = lax.axis_size(axis)
    to_right, to_left = terms[count - step], terms[step]
    if came is not None:
        to_right = to_right + came[0].astype(jnp.float32)
        to_left = to_left + came[1].astype(jnp.float32)
    return (
        right_of(to_right.astype(jnp.bfloat16), axis, 0, step),
        left_of(to_left.astype(jnp.bfloat16), axis, count - step, count),
    )


def halve(blocks, axis, bits):
    for bit in bits:
        sent = {
            k: swap(block.astype(jnp.bfloat16), axis, bit)
            for k, block in blocks.items()
            if k & bit
        }
        blocks = {
            k: block + sent[k | bit].astype(jnp.float32)
            for k, block in blocks.items()
            if not k & bit
        }
    return blocks


def split_heads(array):
    length = array.shape[1]
    return array.reshape(2, length, array.shape[2] // DH, DH).transpose(0, 2, 1, 3)


def join_heads(array):
    length = array.shape[2]
    return array.transpose(0, 2, 1, 3).reshape(2, length, array.shape[1] * DH)


def rms_normalize(attended):
    return attended / jnp.sqrt(jnp.mean(attended * attended, axis=-1, keepdims=True) + epsilon)


def shards(queries, key_rows, value_rows, out_weight, cotangent):
    head_scale = DH ** (-0.5)
    length = queries.shape[1]
    rows_index = lax.broadcasted_iota(jnp.int32, (length, length), 0)
    cols_index = lax.broadcasted_iota(jnp.int32, (length, length), 1)
    lower = rows_index >= cols_index
    groups = lax.axis_size("head")
    group = lax.axis_index("head")
    arrived = {0: (cotangent, cotangent)}
    arrived[1] = gather_step(arrived[0], "head", 1)
    query_heads = split_heads(queries)
    key_heads = split_heads(key_rows)
    value_heads = split_heads(value_rows)
    raw = (
        jnp.einsum("bhtd,bhsd->bhts", query_heads, key_heads, preferred_element_type=jnp.float32)
        * head_scale
    )
    scores = jnp.where(lower, raw, 0.0).astype(jnp.bfloat16)
    local_state = jnp.einsum(
        "bhsd,bhse->bhde", key_heads, value_heads, preferred_element_type=jnp.float32
    )
    state, _ = exclusive_scan(local_state, "ctx", False)
    for step in range(2, groups):
        arrived[step] = gather_step(arrived[step - 1], "head", step)
    state_bf = state.astype(jnp.bfloat16)
    attended = jnp.einsum(
        "bhts,bhsd->bhtd", scores, value_heads, preferred_element_type=jnp.float32
    )
    attended = attended + head_scale * jnp.einsum(
        "bhtd,bhde->bhte", query_heads, state_bf, preferred_element_type=jnp.float32
    )
    normed_flat = join_heads(rms_normalize(attended).astype(jnp.bfloat16))
    width = cotangent.shape[2]
    terms = [
        jnp.einsum(
            "btr,rc->btc",
            normed_flat,
            lax.dynamic_slice_in_dim(out_weight, (group + o) % groups * width, width, 1),
            preferred_element_type=jnp.float32,
        )
        for o in range(groups)
    ]
    came_out = scatter_step(terms, None, "head", 1)
    places = lax.axis_size("ctx")
    core = lax.axis_index("ctx") % 2
    span = groups * width // places
    chips = places // 2
    table = line_order(groups)
    per = chips // groups
    normed_grad = 0.0
    pair_sums = []
    for rank in range(groups):
        block = look_up([row[rank][2] for row in table], group)
        if rank == groups - 1:
            arrived, pair_sums, came_out = lax.optimization_barrier(
                (arrived, pair_sums, came_out)
            )
        grad = pick(arrived, rank, table, group)
        columns = lax.dynamic_slice_in_dim(out_weight, block * width, width, 1)
        normed_grad = normed_grad + jnp.einsum(
            "btc,rc->btr", grad, columns, preferred_element_type=jnp.float32
        )
        for t in range(per):
            theirs, ours = [
                jnp.einsum(
                    "btr,btc->rc",
                    normed_flat,
                    lax.dynamic_slice_in_dim(grad, (2 * t + side) * span, span, 2),
                    preferred_element_type=jnp.float32,
                )
                for side in (1 - core, core)
            ]
            came = swap(theirs.astype(jnp.bfloat16), "ctx", 1)
            pair_sums.append((ours + came.astype(jnp.float32)).astype(jnp.bfloat16))
    pullback = jax.vjp(rms_normalize, attended)[1]
    attended_grad = pullback(split_heads(normed_grad))[0].astype(jnp.bfloat16)
    local_grad_state = jnp.einsum(
        "bhtd,bhte->bhde", query_heads, attended_grad, preferred_element_type=jnp.float32
    )
    pair_sums = jnp.stack(pair_sums)
    chip = lax.axis_index("ctx") // 2
    positions = [[[e[2] for e in row].index(g) for row in table] for g in range(groups)]
    blocks = {}
    for k in range(chips):
        wanted = chip ^ k
        rank = jnp.int32(0)
        for g in range(groups):
            rank = jnp.where(wanted // per == g, look_up(positions[g], group), rank)
        blocks[2 * k] = lax.dynamic_index_in_dim(
            pair_sums, rank * per + wanted % per, 0, False
        ).astype(jnp.float32)
    bits = [1 << i for i in range(1, places.bit_length() - 1)]
    rows = normed_flat.shape[2] // 2
    upper = halve({k: block[:rows] for k, block in blocks.items()}, "ctx", bits[:1])
    downer = halve({k: block[rows:] for k, block in blocks.items()}, "ctx", bits[::-1][:1])
    for step in range(2, groups):
        came_out = scatter_step(terms, came_out, "head", step)
    grad_state, (upper, downer) = exclusive_scan(
        local_grad_state, "ctx", True, (upper, downer)
    )
    grad_state, came_out = lax.optimization_barrier((grad_state, came_out))
    upper = halve(upper, "ctx", bits[1:])
    downer = halve(downer, "ctx", bits[::-1][1:])
    token_factor = (2 * length * places) ** (-0.5)
    weight_grad = jnp.concatenate([upper[0], downer[0]], axis=0) * token_factor
    layer_output = (
        terms[0] + came_out[0].astype(jnp.float32) + came_out[1].astype(jnp.float32)
    ).astype(jnp.bfloat16)
    grad_state_bf = grad_state.astype(jnp.bfloat16)
    raw_grad = (
        jnp.einsum(
            "bhtd,bhsd->bhts", attended_grad, value_heads, preferred_element_type=jnp.float32
        )
        * head_scale
    )
    score_grad = jnp.where(lower, raw_grad, 0.0).astype(jnp.bfloat16)
    query_part = jnp.einsum(
        "bhts,bhsd->bhtd", score_grad, key_heads, preferred_element_type=jnp.float32
    )
    query_part = query_part + head_scale * jnp.einsum(
        "bhte,bhde->bhtd", attended_grad, state_bf, preferred_element_type=jnp.float32
    )
    key_part = jnp.einsum(
        "bhts,bhtd->bhsd", score_grad, query_heads, preferred_element_type=jnp.float32
    )
    key_part = key_part + head_scale * jnp.einsum(
        "bhse,bhde->bhsd", value_heads, grad_state_bf, preferred_element_type=jnp.float32
    )
    value_part = jnp.einsum(
        "bhts,bhte->bhse", scores, attended_grad, preferred_element_type=jnp.float32
    )
    value_part = value_part + head_scale * jnp.einsum(
        "bhsd,bhde->bhse", key_heads, grad_state_bf, preferred_element_type=jnp.float32
    )
    query_grad = join_heads(query_part.astype(jnp.bfloat16))
    key_grad = join_heads(key_part.astype(jnp.bfloat16))
    value_grad = join_heads(value_part.astype(jnp.bfloat16))
    return (layer_output, query_grad, key_grad, value_grad, weight_grad)


def solution(mesh):
    in_specs = (
        P(None, "ctx", "head"),
        P(None, "ctx", "head"),
        P(None, "ctx", "head"),
        P("head", None),
        P(None, "ctx", "head"),
    )
    out_specs = (
        P(None, "ctx", "head"),
        P(None, "ctx", "head"),
        P(None, "ctx", "head"),
        P(None, "ctx", "head"),
        P("head", "ctx"),
    )
    return jax.shard_map(shards, mesh=mesh, in_specs=in_specs, out_specs=out_specs, check_vma=False)
```

```python
import jax
import jax.numpy as jnp
from jax import lax
from jax.sharding import PartitionSpec as P

DH = 128


epsilon = 1e-06


def swap(array, axis, bit):
    count = lax.axis_size(axis)
    return lax.ppermute(array, axis, [(i, i ^ bit) for i in range(count)])


def exclusive_scan(part, axis, reverse, beside=()):
    count = lax.axis_size(axis)
    place = lax.axis_index(axis)
    core = place % 2
    other = swap(part.astype(jnp.bfloat16), axis, 1).astype(jnp.float32)
    total = lax.dynamic_index_in_dim(part + other, core, 0, False)
    before = jnp.zeros_like(total)
    bit = 2
    while bit < count:
        came = swap(total.astype(jnp.bfloat16), axis, bit).astype(jnp.float32)
        mine = (place // bit) % 2
        takes = (mine == 0) if reverse else (mine == 1)
        before = before + jnp.where(takes, came, 0.0)
        total = total + came
        bit *= 2
    before, beside = lax.optimization_barrier((before.astype(jnp.bfloat16), beside))
    came = swap(before, axis, 1)
    first = jnp.where(core == 0, before, came)
    second = jnp.where(core == 0, came, before)
    pairs = jnp.stack([first, second]).astype(jnp.float32)
    takes = (core == 0) if reverse else (core == 1)
    return pairs + jnp.where(takes, other, 0.0), beside


def right_of(array, axis, first, last):
    return lax.ppermute(array, axis, [(i, i + 1) for i in range(first, last)])


def left_of(array, axis, first, last):
    return lax.ppermute(array, axis, [(i, i - 1) for i in range(first, last)])


def line_order(count):
    table = []
    for place in range(count):
        entries = []
        for block in range(count):
            entries.append((abs(block - place), int(block > place), block))
        table.append(sorted(entries))
    return table


def look_up(values, place):
    out = jnp.int32(values[0])
    for i, value in enumerate(values[1:], 1):
        out = jnp.where(place == i, value, out)
    return out


def gather_step(came, axis, step):
    count = lax.axis_size(axis)
    return (
        right_of(came[0], axis, step - 1, count - 1),
        left_of(came[1], axis, 1, count - step + 1),
    )


def pick(arrived, rank, table, place):
    choices = {}
    for i, row in enumerate(table):
        choices.setdefault(row[rank][:2], []).append(i)
    out = None
    for (distance, side), owners in choices.items():
        block = arrived[distance][side]
        if out is None:
            out = block
        else:
            wanted = place == owners[0]
            for owner in owners[1:]:
                wanted = wanted | (place == owner)
            out = jnp.where(wanted, block, out)
    return out


def scatter_step(terms, came, axis, step):
    count = lax.axis_size(axis)
    to_right, to_left = terms[count - step], terms[step]
    if came is not None:
        to_right = to_right + came[0].astype(jnp.float32)
        to_left = to_left + came[1].astype(jnp.float32)
    return (
        right_of(to_right.astype(jnp.bfloat16), axis, 0, step),
        left_of(to_left.astype(jnp.bfloat16), axis, count - step, count),
    )


def halve(blocks, axis, bits):
    for bit in bits:
        sent = {
            k: swap(block.astype(jnp.bfloat16), axis, bit)
            for k, block in blocks.items()
            if k & bit
        }
        blocks = {
            k: block + sent[k | bit].astype(jnp.float32)
            for k, block in blocks.items()
            if not k & bit
        }
    return blocks


def split_heads(array):
    length = array.shape[1]
    return array.reshape(2, length, array.shape[2] // DH, DH).transpose(0, 2, 1, 3)


def join_heads(array):
    length = array.shape[2]
    return array.transpose(0, 2, 1, 3).reshape(2, length, array.shape[1] * DH)


def rms_normalize(attended):
    return attended / jnp.sqrt(jnp.mean(attended * attended, axis=-1, keepdims=True) + epsilon)


def shards(queries, key_rows, value_rows, out_weight, cotangent):
    head_scale = DH ** (-0.5)
    length = queries.shape[1]
    rows_index = lax.broadcasted_iota(jnp.int32, (length, length), 0)
    cols_index = lax.broadcasted_iota(jnp.int32, (length, length), 1)
    lower = rows_index >= cols_index
    groups = lax.axis_size("head")
    group = lax.axis_index("head")
    arrived = {0: (cotangent, cotangent)}
    arrived[1] = gather_step(arrived[0], "head", 1)
    query_heads = split_heads(queries)
    key_heads = split_heads(key_rows)
    value_heads = split_heads(value_rows)
    raw = (
        jnp.einsum("bhtd,bhsd->bhts", query_heads, key_heads, preferred_element_type=jnp.float32)
        * head_scale
    )
    scores = jnp.where(lower, raw, 0.0).astype(jnp.bfloat16)
    local_state = jnp.einsum(
        "bhsd,bhse->bhde", key_heads, value_heads, preferred_element_type=jnp.float32
    )
    state, _ = exclusive_scan(local_state, "ctx", False)
    for step in range(2, groups):
        arrived[step] = gather_step(arrived[step - 1], "head", step)
    state_bf = state.astype(jnp.bfloat16)
    attended = jnp.einsum(
        "bhts,bhsd->bhtd", scores, value_heads, preferred_element_type=jnp.float32
    )
    attended = attended + head_scale * jnp.einsum(
        "bhtd,bhde->bhte", query_heads, state_bf, preferred_element_type=jnp.float32
    )
    normed_flat = join_heads(rms_normalize(attended).astype(jnp.bfloat16))
    width = cotangent.shape[2]
    terms = [
        jnp.einsum(
            "btr,rc->btc",
            normed_flat,
            lax.dynamic_slice_in_dim(out_weight, (group + o) % groups * width, width, 1),
            preferred_element_type=jnp.float32,
        )
        for o in range(groups)
    ]
    came_out = scatter_step(terms, None, "head", 1)
    places = lax.axis_size("ctx")
    core = lax.axis_index("ctx") % 2
    span = groups * width // places
    chips = places // 2
    table = line_order(groups)
    per = chips // groups
    normed_grad = 0.0
    pair_sums = []
    for rank in range(groups):
        block = look_up([row[rank][2] for row in table], group)
        if rank == groups - 1:
            arrived, pair_sums, came_out = lax.optimization_barrier(
                (arrived, pair_sums, came_out)
            )
        grad = pick(arrived, rank, table, group)
        columns = lax.dynamic_slice_in_dim(out_weight, block * width, width, 1)
        normed_grad = normed_grad + jnp.einsum(
            "btc,rc->btr", grad, columns, preferred_element_type=jnp.float32
        )
        for t in range(per):
            theirs, ours = [
                jnp.einsum(
                    "btr,btc->rc",
                    normed_flat,
                    lax.dynamic_slice_in_dim(grad, (2 * t + side) * span, span, 2),
                    preferred_element_type=jnp.float32,
                )
                for side in (1 - core, core)
            ]
            came = swap(theirs.astype(jnp.bfloat16), "ctx", 1)
            pair_sums.append((ours + came.astype(jnp.float32)).astype(jnp.bfloat16))
    pullback = jax.vjp(rms_normalize, attended)[1]
    attended_grad = pullback(split_heads(normed_grad))[0].astype(jnp.bfloat16)
    local_grad_state = jnp.einsum(
        "bhtd,bhte->bhde", query_heads, attended_grad, preferred_element_type=jnp.float32
    )
    pair_sums = jnp.stack(pair_sums)
    chip = lax.axis_index("ctx") // 2
    positions = [[[e[2] for e in row].index(g) for row in table] for g in range(groups)]
    blocks = {}
    for k in range(chips):
        wanted = chip ^ k
        rank = jnp.int32(0)
        for g in range(groups):
            rank = jnp.where(wanted // per == g, look_up(positions[g], group), rank)
        blocks[2 * k] = lax.dynamic_index_in_dim(
            pair_sums, rank * per + wanted % per, 0, False
        ).astype(jnp.float32)
    bits = [1 << i for i in range(1, places.bit_length() - 1)]
    rows = normed_flat.shape[2] // 2
    upper = halve({k: block[:rows] for k, block in blocks.items()}, "ctx", bits[:1])
    downer = halve({k: block[rows:] for k, block in blocks.items()}, "ctx", bits[::-1][:1])
    for step in range(2, groups):
        came_out = scatter_step(terms, came_out, "head", step)
    grad_state, _ = exclusive_scan(
        local_grad_state, "ctx", True, (upper, downer)
    )
    grad_state, came_out = lax.optimization_barrier((grad_state, came_out))
    upper = halve(upper, "ctx", bits[1:])
    downer = halve(downer, "ctx", bits[::-1][1:])
    token_factor = (2 * length * places) ** (-0.5)
    weight_grad = jnp.concatenate([upper[0], downer[0]], axis=0) * token_factor
    layer_output = (
        terms[0] + came_out[0].astype(jnp.float32) + came_out[1].astype(jnp.float32)
    ).astype(jnp.bfloat16)
    grad_state_bf = grad_state.astype(jnp.bfloat16)
    raw_grad = (
        jnp.einsum(
            "bhtd,bhsd->bhts", attended_grad, value_heads, preferred_element_type=jnp.float32
        )
        * head_scale
    )
    score_grad = jnp.where(lower, raw_grad, 0.0).astype(jnp.bfloat16)
    query_part = jnp.einsum(
        "bhts,bhsd->bhtd", score_grad, key_heads, preferred_element_type=jnp.float32
    )
    query_part = query_part + head_scale * jnp.einsum(
        "bhte,bhde->bhtd", attended_grad, state_bf, preferred_element_type=jnp.float32
    )
    key_part = jnp.einsum(
        "bhts,bhtd->bhsd", score_grad, query_heads, preferred_element_type=jnp.float32
    )
    key_part = key_part + head_scale * jnp.einsum(
        "bhse,bhde->bhsd", value_heads, grad_state_bf, preferred_element_type=jnp.float32
    )
    value_part = jnp.einsum(
        "bhts,bhte->bhse", scores, attended_grad, preferred_element_type=jnp.float32
    )
    value_part = value_part + head_scale * jnp.einsum(
        "bhsd,bhde->bhse", key_heads, grad_state_bf, preferred_element_type=jnp.float32
    )
    query_grad = join_heads(query_part.astype(jnp.bfloat16))
    key_grad = join_heads(key_part.astype(jnp.bfloat16))
    value_grad = join_heads(value_part.astype(jnp.bfloat16))
    return (layer_output, query_grad, key_grad, value_grad, weight_grad)


def solution(mesh):
    in_specs = (
        P(None, "ctx", "head"),
        P(None, "ctx", "head"),
        P(None, "ctx", "head"),
        P("head", None),
        P(None, "ctx", "head"),
    )
    out_specs = (
        P(None, "ctx", "head"),
        P(None, "ctx", "head"),
        P(None, "ctx", "head"),
        P(None, "ctx", "head"),
        P("head", "ctx"),
    )
    return jax.shard_map(shards, mesh=mesh, in_specs=in_specs, out_specs=out_specs, check_vma=False)
```
